256 devices in a mesh: leaf: 128 (over z, y_lo, x, core), rhs: 2 (over y_hi).
Axes of the slice: x: 4, y: 4 (y_hi: 2, y_lo: 2; y = y_hi * 2 + y_lo), z: 8, core: 2. Of those that a mesh axis runs over, the one named last changes fastest.
Arguments:
- vectors: bfloat16 [64, 524288], P('rhs', 'leaf'), may hold values from -6 to 6
- leaf_basis: bfloat16 [8192, 64, 64], P('leaf'), may hold values from -0.75 to 0.75
- local_transfer: bfloat16 [16256, 64, 64], P('leaf'), may hold values from -0.5 to 0.5
- coupling: bfloat16 [16256, 4, 64, 64], P('leaf'), may hold values from -0.375 to 0.375
- coupling_source: int32 [16256, 4], P('leaf'), may hold values from 0 to 8191, as said below
- top_transfer: bfloat16 [126, 64, 64], replicated, may hold values from -0.5 to 0.5
- top_coupling: bfloat16 [512, 64, 64], P('leaf'), may hold values from -0.75 to 0.75
- top_target: int32 [512], P('leaf'), may hold values from 2 to 127, as said below
- top_source: int32 [512], P('leaf'), may hold values from 2 to 127, as said below
- near_blocks: bfloat16 [8192, 8, 64, 64], P('leaf', 'rhs'), may hold values from -0.25 to 0.25
- near_source: int32 [8192, 8], P('leaf', 'rhs'), may hold values from 0 to 8191, as said below
Outputs:
- product: bfloat16 [64, 524288], P('rhs', 'leaf')
The draws below stay inside these ranges and needn't reach their ends.
Inputs may be any that keep to these rules, and one draw needn't show every extreme that they name: `coupling_source`: entry k of a row names a node of that row's level other than the row's own node, at most n away from it along the level, where n is the level's nodes of one subtree; entry 0 is the node's sibling. near_source[t, 0] is t; every other entry of row t lies within 64 leaves of t and differs from t. `top_target`: an upper heap node; top_target[b] and top_source[b] are different nodes of the same upper level. `top_source`: an upper heap node of the same level as top_target[b], never equal to it.
All inputs are finite; a program needn't handle non-finite values.
Results may differ from the reference program's by a relative error of at most 0.025.
Values may be sent and summed in bfloat16 or wider, within the bound.
No kernel may reach another device: no remote copies, remote signals or barrier semaphores. Data moves between devices by JAX's collectives and lax.ppermute only.
A program may use at most 128 MiB of HBM per device.

```python
import jax
import jax.numpy as jnp
import numpy as np
from jax import lax

LEAF = 64
RANK = 64
RHS = 64
K = 4
NEAR = 8
K_TOP = 4
LEAF_DEV = 64
LEAVES = 8192
POINTS = 524288
NODES_DEV = 127
N_LEAF = 128


def reflect_offsets(key, target, reach, limit, slots):
    key_size, key_sign = jax.random.split(key)
    magnitude = jax.random.randint(key_size, (target.shape[0], slots), 0, 1 << 20) % reach[:, None] + 1
    upward = jax.random.randint(key_sign, (target.shape[0], slots), 0, 2)
    offset = jnp.where(upward == 1, magnitude, -magnitude)
    candidate = target[:, None] + offset
    inside = (candidate >= 0) & (candidate < limit[:, None])
    return jnp.where(inside, candidate, target[:, None] - offset).astype(jnp.int32)


def draw_coupling_source(key, part):
    key = jax.random.fold_in(key, 11)
    node_total = 2 * LEAF_DEV - 1
    per_level = []
    position = []
    node_count = LEAF_DEV
    while node_count >= 1:
        per_level.append(np.full(node_count, node_count))
        position.append(np.arange(node_count))
        node_count //= 2
    per_level = np.concatenate(per_level)
    position = np.concatenate(position)
    row_ids = np.arange(N_LEAF * node_total)
    per_row = per_level[row_ids % node_total]
    target_np = row_ids // node_total * per_row + position[row_ids % node_total]
    target = jnp.asarray(target_np, jnp.int32)
    reach = jnp.asarray(per_row, jnp.int32)
    limit = jnp.asarray(per_row * N_LEAF, jnp.int32)
    chosen = reflect_offsets(key, target, reach, limit, K)
    sibling = jnp.where(target % 2 == 0, target + 1, target - 1)
    return chosen.at[:, 0].set(sibling)


def draw_near_source(key, part):
    key = jax.random.fold_in(key, 12)
    target = jnp.arange(LEAVES, dtype=jnp.int32)
    reach = jnp.full((LEAVES,), LEAF_DEV, jnp.int32)
    limit = jnp.full((LEAVES,), LEAVES, jnp.int32)
    chosen = reflect_offsets(key, target, reach, limit, NEAR)
    return chosen.at[:, 0].set(target)


def upper_pairs(key):
    block_total = N_LEAF * K_TOP
    key_target, key_offset = jax.random.split(jax.random.fold_in(key, 21))
    target = jax.random.randint(key_target, (block_total,), 2, N_LEAF)
    lowest = jnp.full((block_total,), 2, jnp.int32)
    power = 4
    while power < N_LEAF:
        lowest = jnp.where(target >= power, power, lowest)
        power *= 2
    offset = jax.random.randint(key_offset, (block_total,), 0, 1 << 20) % (lowest - 1) + 1
    source = lowest + (target - lowest + offset) % lowest
    target = target.at[0].set(2).at[1].set(N_LEAF - 1)
    source = source.at[0].set(3).at[1].set(N_LEAF - 2)
    return (target.astype(jnp.int32), source.astype(jnp.int32))


def draw_top_target(key, part):
    chosen = upper_pairs(key)
    return chosen[0]


def draw_top_source(key, part):
    chosen = upper_pairs(key)
    return chosen[1]


def steps_of(rng, dims, cuts, low, high):
    factor_of, own = 1.0, jax.random.fold_in(rng, 6)
    for dim, parts in cuts:
        heights = jnp.exp(jax.random.uniform(jax.random.fold_in(own, dim), (parts,), jnp.float32, low / len(cuts), high / len(cuts)))
        factor_of = factor_of * jnp.repeat(heights, dims[dim] // parts).reshape([-1 if axis == dim else 1 for axis in range(len(dims))])
    return factor_of


def bell_draw(rng, extent, width, most, cuts=(), kind=jnp.bfloat16):
    level = steps_of(rng, extent, cuts, -0.22, 0.18) if cuts else 1.0
    result = jax.random.normal(rng, extent, jnp.float32) * width * level
    return jnp.minimum(jnp.maximum(result, -most), most).astype(kind)


def setup_inputs(seed: int = 0) -> dict:
    seeds = jax.random.split(jax.random.key(seed), 12)
    vectors = bell_draw(seeds[0], (RHS, POINTS), 1.0, 6.0, ((0, 2), (1, 128)))
    leaf_basis = bell_draw(seeds[1], (LEAVES, LEAF, RANK), LEAF ** -0.5, 0.75, ((0, 128),))
    local_transfer = bell_draw(seeds[2], (N_LEAF * NODES_DEV, RANK, RANK), (2 * RANK) ** -0.5, 0.5, ((0, 128),))
    coupling = bell_draw(seeds[3], (N_LEAF * NODES_DEV, K, RANK, RANK), (K * RANK) ** -0.5, 0.375, ((0, 128),))
    coupling_source = draw_coupling_source(jax.random.fold_in(seeds[11], 71), 0)
    top_transfer = bell_draw(seeds[5], (N_LEAF - 2, RANK, RANK), (2 * RANK) ** -0.5, 0.5)
    top_coupling = bell_draw(seeds[6], (N_LEAF * K_TOP, RANK, RANK), RANK ** -0.5, 0.75, ((0, 128),))
    top_target = draw_top_target(jax.random.fold_in(seeds[11], 71), 0)
    top_source = draw_top_source(jax.random.fold_in(seeds[11], 71), 0)
    near_blocks = bell_draw(seeds[9], (LEAVES, NEAR, LEAF, LEAF), (NEAR * LEAF) ** -0.5, 0.25, ((0, 128), (1, 2)))
    near_source = draw_near_source(jax.random.fold_in(seeds[11], 71), 0)
    return {"vectors": vectors, "leaf_basis": leaf_basis, "local_transfer": local_transfer, "coupling": coupling, "coupling_source": coupling_source, "top_transfer": top_transfer, "top_coupling": top_coupling, "top_target": top_target, "top_source": top_source, "near_blocks": near_blocks, "near_source": near_source}


full_precision = lax.Precision.HIGHEST


def level_table(leaf_count):
    layout = []
    first_node = 0
    node_count = leaf_count
    while node_count >= 1:
        layout.append((first_node, node_count))
        first_node += node_count
        node_count //= 2
    return layout


def level_rows(stacked, first_node, node_count):
    picked = stacked[:, first_node:first_node + node_count]
    return picked.reshape((stacked.shape[0] * node_count,) + picked.shape[2:])


def descend(upper_field, top_transfer, root_count):
    upper_down = upper_field[:, 2:4]
    level_size = 4
    while level_size < root_count:
        parents = jnp.repeat(upper_down, 2, axis=1)
        transfer_rows = top_transfer[level_size - 2:2 * level_size - 2].astype(jnp.float32)
        upper_down = upper_field[:, level_size:2 * level_size] + jnp.einsum('rhb,hab->rha', parents, transfer_rows, precision=full_precision)
        level_size *= 2
    return upper_down


def reference(vectors, leaf_basis, local_transfer, coupling, coupling_source, top_transfer, top_coupling, top_target, top_source, near_blocks, near_source):
    layout = level_table(LEAF_DEV)
    node_total = 2 * LEAF_DEV - 1
    leaf_points = vectors.reshape(RHS, LEAVES, LEAF)
    transfer = local_transfer.reshape(N_LEAF, node_total, RANK, RANK)
    blocks = coupling.reshape(N_LEAF, node_total, K, RANK, RANK)
    sources = coupling_source.reshape(N_LEAF, node_total, K)
    coefficients = [jnp.einsum('rip,ipk->rik', leaf_points.astype(jnp.float32), leaf_basis.astype(jnp.float32), precision=full_precision).astype(jnp.bfloat16)]
    for height in range(1, len(layout)):
        first_node, node_count = layout[height - 1]
        transfer_rows = level_rows(transfer, first_node, node_count).astype(jnp.float32)
        lifted = jnp.einsum('rik,ikm->rim', coefficients[-1].astype(jnp.float32), transfer_rows, precision=full_precision)
        coefficients.append(lifted.reshape(RHS, -1, 2, RANK).sum(axis=2).astype(jnp.bfloat16))
    fields = []
    for height in range(len(layout)):
        first_node, node_count = layout[height]
        level_blocks = level_rows(blocks, first_node, node_count)
        level_sources = level_rows(sources, first_node, node_count)
        summed = jnp.zeros((RHS, N_LEAF * node_count, RANK), jnp.float32)
        for slot in range(K):
            picked = jnp.take(coefficients[height], level_sources[:, slot], axis=1).astype(jnp.float32)
            summed = summed + jnp.einsum('rtm,tmn->rtn', picked, level_blocks[:, slot].astype(jnp.float32), precision=full_precision)
        fields.append(summed)
    root_transfer = transfer[:, node_total - 1].astype(jnp.float32)
    root_term = jnp.einsum('rdk,dkm->rdm', coefficients[-1].astype(jnp.float32), root_transfer, precision=full_precision)
    upper = [root_term.reshape(RHS, N_LEAF // 2, 2, RANK).sum(axis=2).astype(jnp.bfloat16)]
    level_size = N_LEAF // 2
    while level_size > 2:
        transfer_rows = top_transfer[level_size - 2:2 * level_size - 2].astype(jnp.float32)
        lifted = jnp.einsum('rhk,hkm->rhm', upper[0].astype(jnp.float32), transfer_rows, precision=full_precision)
        upper.insert(0, lifted.reshape(RHS, level_size // 2, 2, RANK).sum(axis=2).astype(jnp.bfloat16))
        level_size //= 2
    heap_coef = jnp.concatenate([jnp.zeros((RHS, 2, RANK), jnp.bfloat16)] + upper, axis=1)
    picked = jnp.take(heap_coef, top_source, axis=1).astype(jnp.float32)
    contrib = jnp.einsum('rbm,bmn->rbn', picked, top_coupling.astype(jnp.float32), precision=full_precision)
    upper_field = jnp.zeros((RHS, N_LEAF, RANK), jnp.float32).at[:, top_target].add(contrib)
    upper_down = descend(upper_field, top_transfer, N_LEAF)
    parents = jnp.repeat(upper_down, 2, axis=1)
    descent = (fields[-1] + jnp.einsum('rdb,dab->rda', parents, root_transfer, precision=full_precision)).astype(jnp.bfloat16)
    for height in range(len(layout) - 2, -1, -1):
        first_node, node_count = layout[height]
        transfer_rows = level_rows(transfer, first_node, node_count).astype(jnp.float32)
        parents = jnp.repeat(descent, 2, axis=1).astype(jnp.float32)
        descent = (fields[height] + jnp.einsum('rtb,tab->rta', parents, transfer_rows, precision=full_precision)).astype(jnp.bfloat16)
    far_part = jnp.einsum('rik,ipk->rip', descent.astype(jnp.float32), leaf_basis.astype(jnp.float32), precision=full_precision)
    near_sum = jnp.zeros((RHS, LEAVES, LEAF), jnp.float32)
    for slot in range(NEAR):
        picked = jnp.take(leaf_points, near_source[:, slot], axis=1).astype(jnp.float32)
        near_sum = near_sum + jnp.einsum('riq,ipq->rip', picked, near_blocks[:, slot].astype(jnp.float32), precision=full_precision)
    return (far_part + near_sum).reshape(RHS, POINTS).astype(jnp.bfloat16)
```

```python
import functools

import jax
import jax.numpy as jnp
import numpy as np
from jax import lax
from jax.experimental import pallas as pl
from jax.experimental.pallas import tpu as pltpu
from jax.sharding import PartitionSpec as P

BF = jnp.bfloat16
F32 = jnp.float32
VMEM_LIMIT = 44 * 1024 * 1024

NODES = 128
SIZES = (64, 32, 16, 8, 4, 2, 1)
FIRST = (0, 64, 96, 112, 120, 124, 126)
SLOT = (0, 32, 48, 56, 60, 62, 63)
R = 32


def _nn(a, b):
    return lax.dot_general(a, b, (((1,), (0,)), ((), ())), preferred_element_type=F32)


def _nt(a, b):
    return lax.dot_general(a, b, (((1,), (1,)), ((), ())), preferred_element_type=F32)


def _low(rows):
    return lax.broadcasted_iota(jnp.int32, (rows, 128), 1) < 64


def _eye(lanes):
    row = lax.broadcasted_iota(jnp.int32, (128, lanes), 0)
    col = lax.broadcasted_iota(jnp.int32, (128, lanes), 1)
    return jnp.where(row == col, 1.0, 0.0).astype(BF)


def _pick_half(low, half, x, zero):
    return jnp.where(low == (half == 0), x, zero)


def _roll(x):
    return pltpu.roll(x, 64, 1)


def _unstack(raw_ref, wide, count):
    eye = _eye(raw_ref.shape[2])

    def body(k, carry):
        block = raw_ref[k]
        both = jnp.concatenate([block, block], axis=0)
        wide[pl.ds(k, NODES, stride=64), :] = _nt(eye, both)
        return carry

    lax.fori_loop(0, count, body, 0, unroll=8)


def up_kernel(v_ref, basis_ref, raw_ref, msg_ref, root_ref, wide_ref, wide):
    _unstack(raw_ref, wide, 64)

    def narrow(i, carry):
        rows = pl.ds(pl.multiple_of(i * 512, 512), 512)
        wide_ref[rows, :] = wide[rows, :].astype(BF)
        return carry

    lax.fori_loop(0, 16, narrow, 0, unroll=2)
    low = _low(R)
    zero = jnp.zeros((R, 128), BF)
    for p in range(32):
        v = v_ref[:, 128 * p : 128 * p + 128]
        msg_ref[64 + p] = v
        both = jnp.concatenate([jnp.where(low, v, zero), jnp.where(low, zero, v)], axis=0)
        y = _nn(both, basis_ref[2 * p : 2 * p + 2].reshape(128, 64))
        msg_ref[p] = jnp.concatenate([y[:R], y[R:]], axis=1).astype(BF)
    for level in range(1, 7):
        for s in range(max(1, SIZES[level] // 2)):
            parts = []
            for q in (2 * s, 2 * s + 1)[: min(2, SIZES[level])]:
                row = (FIRST[level - 1] + 2 * q) * 64
                parts.append(_nn(msg_ref[SLOT[level - 1] + q], wide_ref[row : row + 128, :]))
            value = parts[0] if len(parts) == 1 else jnp.where(low, parts[0], parts[1])
            msg_ref[SLOT[level] + s] = value.astype(BF)
    root_ref[...] = _nn(msg_ref[63][:, :64], wide_ref[126 * 64 : 127 * 64, :])


def pack_kernel(core_ref, mine_ref, other_ref, out_ref):
    core = core_ref[0]
    total = mine_ref[...] + other_ref[...]
    half = jnp.where(core == 0, total[:16], total[16:])
    packed = jnp.where(_low(8), half[:8], half[8:]).astype(BF)
    out_ref[...] = jnp.broadcast_to(packed[None], out_ref.shape)


def upper_kernel(ids_ref, ids2_ref, gathered_ref, raw_ref, blocks_ref, blocks2_ref, out_ref, wide, coef, field):
    _unstack(raw_ref, wide, 64)
    low8, low = _low(8), _low(16)
    zero = jnp.zeros((16, 128), BF)
    zero32 = jnp.zeros((16, 128), F32)
    for s in range(32):
        a, b = gathered_ref[2 * s].astype(F32), gathered_ref[2 * s + 1].astype(F32)
        top = jnp.where(low8, a, _roll(b))
        bottom = jnp.where(low8, _roll(a), b)
        coef[32 + s] = jnp.concatenate([top, bottom], axis=0).astype(BF)
    field[...] = jnp.zeros_like(field)
    size = 32
    while size >= 2:
        for s in range(size // 2, size):
            parts = []
            for h in (2 * s, 2 * s + 1):
                row = (2 * h - 2) * 64
                parts.append(_nn(coef[h], wide[row : row + 128, :].astype(BF)))
            coef[s] = jnp.where(low, parts[0], parts[1]).astype(BF)
        size //= 2
    for b in range(8):
        ids, blocks, k = (ids_ref, blocks_ref, b) if b < 4 else (ids2_ref, blocks2_ref, b - 4)
        target, source = ids[k], ids[4 + k]
        block = blocks[k]
        block = jnp.concatenate([block, block], axis=0)
        block = jnp.concatenate([block, block], axis=1)
        x = _pick_half(low, source % 2, coef[source // 2], zero)
        field[target // 2] += _pick_half(low, target % 2, _nn(x, block), zero32)
    for h in range(2, 64):
        row = (2 * h - 2) * 64
        x = _pick_half(low, h % 2, field[h // 2].astype(BF), zero)
        field[h] += _nt(x, wide[row : row + 128, :].astype(BF))
    for s in range(32):
        x = field[32 + s]
        top, bottom = x[:8], x[8:]
        out_ref[2 * s] = jnp.where(low8, top, _roll(bottom)).astype(BF)
        out_ref[2 * s + 1] = jnp.where(low8, _roll(top), bottom).astype(BF)


def near_kernel(ids_ref, left_ref, own_ref, right_ref, other_ref, blocks_ref, mine_out, other_out, leaves):
    step = pl.program_id(0)

    @pl.when(step == 0)
    def _():
        for part, ref in enumerate((left_ref, own_ref, right_ref)):

            def body(s, carry, ref=ref, part=part):
                x, y = ref[64 + s], other_ref[32 * part + s]
                z = jnp.concatenate([x, y], axis=0)
                e = 64 * part + 2 * s
                leaves[e] = z[:, :64]
                leaves[e + 1] = z[:, 64:]
                return carry

            lax.fori_loop(0, 32, body, 0, unroll=4)

    for p in range(4):
        parts = []
        for i in (2 * p, 2 * p + 1):
            leaf = step * 8 + i
            total = _nt(leaves[ids_ref[0, leaf]], blocks_ref[i, 0])
            for j in range(1, 4):
                total += _nt(leaves[ids_ref[j, leaf]], blocks_ref[i, j])
            parts.append(total)
        pair = jnp.concatenate(parts, axis=1)
        mine_out[:, 128 * p : 128 * p + 128] = pair[:R]
        other_out[:, 128 * p : 128 * p + 128] = pair[R:].astype(BF)


CHUNK = 8


def field_kernel(ids_ref, left_ref, own_ref, right_ref, raw_ref, out_ref, wide, coef):
    step = pl.program_id(0)
    eye = _eye(raw_ref.shape[3])
    low = _low(R)
    for k in range(2):

        def body(m, carry, k=k):
            both = jnp.concatenate([raw_ref[k, m], raw_ref[k + 2, m]], axis=0)
            row = k * 64 + step * CHUNK + m
            wide[pl.ds(row, NODES, stride=128), :] = _nt(eye, both)
            return carry

        lax.fori_loop(0, CHUNK, body, 0, unroll=True)

    @pl.when(step == 64 // CHUNK - 1)
    def _():
        for part, ref in enumerate((left_ref, own_ref, right_ref)):

            def spread(s, carry, ref=ref, part=part):
                x = ref[s]
                y = jnp.concatenate([x[:, 64:], x[:, :64]], axis=1)
                coef[part * NODES + 2 * s] = jnp.where(low, x, y)
                coef[part * NODES + 2 * s + 1] = jnp.where(low, y, x)
                return carry

            lax.fori_loop(0, 64, spread, 0, unroll=4)

        def node(t):
            a = jnp.where(low, coef[ids_ref[0, t]], coef[ids_ref[1, t]])
            b = jnp.where(low, coef[ids_ref[2, t]], coef[ids_ref[3, t]])
            rows = pl.ds(pl.multiple_of(t * 128, 128), 128)
            y = _nn(jnp.concatenate([a, b], axis=0), wide[rows, :].astype(BF))
            return y[:R], y[R:]

        def pair(s, carry):
            a0, b0 = node(2 * s)
            a1, b1 = node(2 * s + 1)
            out_ref[s] = jnp.where(low, a0, b1) + _roll(jnp.where(low, a1, b0))
            return carry

        lax.fori_loop(0, 63, pair, 0, unroll=3)
        a0, b0 = node(126)
        out_ref[63] = a0 + _roll(b0)


def down_kernel(core_ref, mine_ref, other_ref, field_ref, wide_ref, basis_ref, near_ref, near2_ref, out_ref, down):
    core = core_ref[0]
    low = _low(R)
    zero = jnp.zeros((R, 128), BF)
    first = jnp.where(core == 0, mine_ref[...], other_ref[...])
    second = jnp.where(core == 0, other_ref[...], mine_ref[...])
    upper = jnp.concatenate([first, _roll(first), second, _roll(second)], axis=0)
    upper = jnp.where(low, upper, 0.0).astype(BF)
    root = field_ref[63][:, :64] + _nt(upper, wide_ref[126 * 64 : 127 * 64, :])
    down[63] = jnp.concatenate([root, root], axis=1).astype(BF)
    for level in range(5, -1, -1):
        for q in range(SIZES[level + 1]):
            row = (FIRST[level] + 2 * q) * 64
            x = _pick_half(low, q % 2, down[SLOT[level + 1] + q // 2], zero)
            s = SLOT[level] + q
            down[s] = (field_ref[s] + _nt(x, wide_ref[row : row + 128, :])).astype(BF)
    for p in range(32):
        d = down[p]
        both = jnp.concatenate([d[:, :64], d[:, 64:]], axis=0)
        y = _nt(both, basis_ref[2 * p : 2 * p + 2].reshape(128, 64))
        lanes = slice(128 * p, 128 * p + 128)
        total = jnp.where(low, y[:R], y[R:]) + near_ref[:, lanes] + near2_ref[:, lanes].astype(F32)
        out_ref[:, lanes] = total.astype(BF)


def _call(body, outs, ins, scratch=(), grid=None, out_specs=None, name=None, flops=0, moved=0):
    single = not isinstance(outs, (list, tuple))
    shapes = [outs] if single else list(outs)
    extra = {}
    if grid is not None:
        extra["grid"] = grid
    vm = pl.BlockSpec(memory_space=pltpu.VMEM)
    specs = out_specs if out_specs is not None else [vm] * len(shapes)
    return pl.pallas_call(
        body,
        out_shape=shapes[0] if single else tuple(shapes),
        in_specs=ins,
        out_specs=specs[0] if single else tuple(specs),
        scratch_shapes=list(scratch),
        compiler_params=pltpu.CompilerParams(vmem_limit_bytes=VMEM_LIMIT),
        cost_estimate=pl.CostEstimate(flops=flops, bytes_accessed=moved, transcendentals=0),
        name=name,
        **extra,
    )


def shards(
    vectors,
    leaf_basis,
    local_transfer,
    coupling,
    coupling_source,
    top_transfer,
    top_coupling,
    top_target,
    top_source,
    near_blocks,
    near_source,
):
    n_leaf = lax.axis_size("leaf")
    me = lax.axis_index("leaf")
    core = (me % 2).astype(jnp.int32).reshape(1)
    vm = pl.BlockSpec(memory_space=pltpu.VMEM)
    sm = pl.BlockSpec(memory_space=pltpu.SMEM)
    S = jax.ShapeDtypeStruct
    pair = [(i, i ^ 1) for i in range(n_leaf)]
    up = [(i, i + 1) for i in range(n_leaf - 1)]
    back = [(i + 1, i) for i in range(n_leaf - 1)]
    swap = [(0, 1), (1, 0)]
    groups = [[2 * i + c for i in range(n_leaf // 2)] for c in range(2)]

    width = np.concatenate([np.full(n, n) for n in SIZES])
    first = np.concatenate([np.full(n, f) for n, f in zip(SIZES, FIRST)])
    shift = np.log2(width).astype(np.int32)
    width, first = jnp.asarray(width, jnp.int32)[None], jnp.asarray(first, jnp.int32)[None]
    shift = jnp.asarray(shift)[None]
    seen = coupling_source.T - (me - 1) * width
    field_ids = lax.shift_right_logical(seen, shift) * NODES + first + (seen & (width - 1))
    near_ids = near_source.T - (me - 1) * 64

    top_ids = jnp.concatenate([top_target, top_source])
    top_ids2 = lax.ppermute(top_ids, "leaf", pair)
    top_coupling2 = lax.ppermute(top_coupling, "leaf", pair)

    msg, root, wide = _call(
        up_kernel,
        (S((96, R, 128), BF), S((R, 128), F32), S((NODES * 64, 128), BF)),
        [vm, vm, vm],
        [pltpu.VMEM((NODES * 64, 128), F32)],
        name="up",
    )(vectors, leaf_basis, jnp.transpose(local_transfer, (1, 2, 0)))

    root2 = lax.ppermute(root, "leaf", pair)
    send = _call(pack_kernel, S((n_leaf // 2, 8, 128), BF), [sm, vm, vm], name="pack")(core, root, root2)
    before = lax.ppermute(msg, "leaf", up)
    after = lax.ppermute(msg, "leaf", back)
    gathered = lax.all_to_all(send, "leaf", 0, 0, tiled=True, axis_index_groups=groups)

    points = jnp.concatenate([before[64:], msg[64:], after[64:]], axis=0)
    points2 = lax.ppermute(points, "rhs", swap)

    partial = _call(
        upper_kernel,
        S((n_leaf // 2, 8, 128), BF),
        [sm, sm, vm, vm, vm, vm],
        [
            pltpu.VMEM((NODES * 64, 128), F32),
            pltpu.VMEM((64, 16, 128), BF),
            pltpu.VMEM((64, 16, 128), F32),
        ],
        name="upper",
    )(top_ids, top_ids2, gathered, jnp.transpose(top_transfer, (1, 2, 0)), top_coupling, top_coupling2)
    parts = lax.all_to_all(partial, "leaf", 0, 0, tiled=True, axis_index_groups=groups)
    mine = jnp.sum(parts.astype(F32), axis=0)
    other = lax.ppermute(mine, "leaf", pair)

    whole = lambda shape: pl.BlockSpec(shape, lambda i: (0,) * len(shape))
    near_mine, near_send = _call(
        near_kernel,
        (S((R, 4096), F32), S((R, 4096), BF)),
        [sm] + [whole((96, R, 128))] * 4 + [pl.BlockSpec((8, 4, 64, 64), lambda i: (i, 0, 0, 0))],
        [pltpu.VMEM((192, 64, 64), BF)],
        grid=(8,),
        out_specs=[pl.BlockSpec((R, 512), lambda i: (0, i))] * 2,
        name="near",
    )(near_ids, before, msg, after, points2, near_blocks)
    near_other = lax.ppermute(near_send, "rhs", swap)

    fields = _call(
        field_kernel,
        S((64, R, 128), F32),
        [sm]
        + [whole((96, R, 128))] * 3
        + [pl.BlockSpec((4, CHUNK, 64, 127), lambda i: (0, i, 0, 0))],
        [pltpu.VMEM((NODES * 128, 128), F32), pltpu.VMEM((3 * NODES, R, 128), BF)],
        grid=(64 // CHUNK,),
        out_specs=[whole((64, R, 128))],
        name="field",
    )(field_ids, before, msg, after, jnp.transpose(coupling, (1, 2, 3, 0)))

    return _call(
        down_kernel,
        S((R, 4096), BF),
        [sm] + [vm] * 7,
        [pltpu.VMEM((64, R, 128), BF)],
        name="down",
    )(core, mine, other, fields, wide, leaf_basis, near_mine, near_other)


def solution(mesh):
    placed = (
        P("rhs", "leaf"),
        P("leaf", None, None),
        P("leaf", None, None),
        P("leaf", None, None, None),
        P("leaf", None),
        P(),
        P("leaf", None, None),
        P("leaf"),
        P("leaf"),
        P("leaf", "rhs", None, None),
        P("leaf", "rhs"),
    )
    return jax.shard_map(
        shards, mesh=mesh, in_specs=placed, out_specs=P("rhs", "leaf"), check_vma=False
    )
```

```python
import jax
import jax.numpy as jnp
from jax import lax
from jax.experimental import pallas as pl
from jax.experimental.pallas import tpu as pltpu
from jax.sharding import PartitionSpec as P

BF = jnp.bfloat16
F32 = jnp.float32
MIB = 1024 * 1024

NODES = 128
SIZES = (64, 32, 16, 8, 4, 2, 1)
FIRST = (0, 64, 96, 112, 120, 124, 126)
SLOT = (0, 32, 48, 56, 60, 62, 63)
R = 32


def _nn(a, b):
    return lax.dot_general(a, b, (((1,), (0,)), ((), ())), preferred_element_type=F32)


def _nt(a, b):
    return lax.dot_general(a, b, (((1,), (1,)), ((), ())), preferred_element_type=F32)


def _low(rows):
    return lax.broadcasted_iota(jnp.int32, (rows, 128), 1) < 64


def _eye(lanes):
    row = lax.broadcasted_iota(jnp.int32, (128, lanes), 0)
    col = lax.broadcasted_iota(jnp.int32, (128, lanes), 1)
    return jnp.where(row == col, 1.0, 0.0).astype(BF)


def _pick_half(low, half, x, zero):
    return jnp.where(low == (half == 0), x, zero)


def _roll(x):
    return pltpu.roll(x, 64, 1)


PITCH = 72
PITCH_FIELD = 136


def _fetch(sems, *moves):
    copies = [pltpu.make_async_copy(src, dst, sems.at[i]) for i, (src, dst) in enumerate(moves)]
    for copy in copies:
        copy.start()
    return copies


def _chunks(src, dst, parts):
    size = src.shape[0] // parts
    return [
        (src.at[i * size : (i + 1) * size], dst.at[i * size : (i + 1) * size]) for i in range(parts)
    ]


def _unstack(raw_ref, wide, copies):
    eye = _eye(raw_ref.shape[2])
    size = 64 // len(copies)
    for k in range(64):
        if k % size == 0:
            copies[k // size].wait()
        block = raw_ref[k]
        both = jnp.concatenate([block, block], axis=0)
        wide[pl.ds(k, NODES, stride=PITCH), :] = _nt(eye, both)


def _narrow(wide, out_ref, nodes):
    for t in nodes:
        out_ref[64 * t : 64 * t + 64, :] = wide[PITCH * t : PITCH * t + 64, :].astype(BF)


def up_kernel(
    v_hbm, basis_hbm, raw_hbm, msg_ref, root_ref, wide_hbm, v_ref, basis_ref, raw_ref, wide, wide_ref, sems, out_sems
):
    copies = _fetch(sems, (v_hbm, v_ref), (basis_hbm, basis_ref), *_chunks(raw_hbm, raw_ref, 1))
    low = _low(R)
    zero = jnp.zeros((R, 128), BF)
    copies[0].wait()
    copies[1].wait()
    for p in range(32):
        v = v_ref[:, 128 * p : 128 * p + 128]
        msg_ref[64 + p] = v
        both = jnp.concatenate([jnp.where(low, v, zero), jnp.where(low, zero, v)], axis=0)
        y = _nn(both, basis_ref[2 * p : 2 * p + 2].reshape(128, 64))
        msg_ref[p] = jnp.concatenate([y[:R], y[R:]], axis=1).astype(BF)
    _unstack(raw_ref, wide, copies[2:])
    _narrow(wide, wide_ref, range(NODES))
    out = _fetch(out_sems, (wide_ref, wide_hbm))
    for level in range(1, 7):
        for s in range(max(1, SIZES[level] // 2)):
            parts = []
            for q in (2 * s, 2 * s + 1)[: min(2, SIZES[level])]:
                row = (FIRST[level - 1] + 2 * q) * 64
                parts.append(_nn(msg_ref[SLOT[level - 1] + q], wide_ref[row : row + 128, :]))
            value = parts[0] if len(parts) == 1 else jnp.where(low, parts[0], parts[1])
            msg_ref[SLOT[level] + s] = value.astype(BF)
    root_ref[...] = _nn(msg_ref[63][:, :64], wide_ref[126 * 64 : 127 * 64, :])
    out[0].wait()


def pack_kernel(me_ref, mine_ref, other_ref, blocks_ref, target_ref, source_ref, out_ref):
    core = me_ref[0] % 2
    total = mine_ref[...] + other_ref[...]
    half = jnp.where(core == 0, total[:16], total[16:])
    packed = jnp.where(_low(8), half[:8], half[8:]).astype(BF)
    out_ref[...] = jnp.broadcast_to(packed[None], out_ref.shape)


def sum_kernel(parts_ref, out_ref):
    out_ref[...] = jnp.sum(parts_ref[...].astype(F32), axis=0)


def bundle_kernel(msg_ref, other_ref, done_ref, gathered_ref, out_ref):
    for s in range(32):
        out_ref[s] = other_ref[:, 128 * s : 128 * s + 128]


def top_kernel(raw_hbm, send_hbm, wide_hbm, done_ref, raw_ref, wide, wide_ref, sems, out_sems):
    copies = _fetch(sems, (raw_hbm, raw_ref))
    _unstack(raw_ref, wide, copies)
    _narrow(wide, wide_ref, range(NODES))
    out = _fetch(out_sems, (wide_ref, wide_hbm))
    done_ref[...] = jnp.zeros((8, 128), F32)
    out[0].wait()


def upper_kernel(
    target_ref, source_ref, target2_ref, source2_ref, gathered_ref, wide_hbm, blocks_hbm, blocks2_hbm, out_ref, wide, blocks_ref, coef, field, sems
):
    copies = _fetch(
        sems,
        (wide_hbm, wide),
        (blocks_hbm, blocks_ref.at[0:4]),
        (blocks2_hbm, blocks_ref.at[4:8]),
    )
    low8, low = _low(8), _low(16)
    zero = jnp.zeros((16, 128), BF)
    zero32 = jnp.zeros((16, 128), F32)
    for s in range(32):
        a, b = gathered_ref[2 * s].astype(F32), gathered_ref[2 * s + 1].astype(F32)
        top = jnp.where(low8, a, _roll(b))
        bottom = jnp.where(low8, _roll(a), b)
        coef[32 + s] = jnp.concatenate([top, bottom], axis=0).astype(BF)
    field[...] = jnp.zeros_like(field)
    copies[0].wait()
    size = 32
    while size >= 2:
        for s in range(size // 2, size):
            parts = []
            for h in (2 * s, 2 * s + 1):
                row = (2 * h - 2) * 64
                parts.append(_nn(coef[h], wide[row : row + 128, :]))
            coef[s] = jnp.where(low, parts[0], parts[1]).astype(BF)
        size //= 2
    copies[1].wait()
    copies[2].wait()
    for b in range(8):
        target = target_ref[b] if b < 4 else target2_ref[b - 4]
        source = source_ref[b] if b < 4 else source2_ref[b - 4]
        block = blocks_ref[b]
        block = jnp.concatenate([block, block], axis=0)
        block = jnp.concatenate([block, block], axis=1)
        x = _pick_half(low, source % 2, coef[source // 2], zero)
        field[target // 2] += _pick_half(low, target % 2, _nn(x, block), zero32)
    for h in range(2, 64):
        row = (2 * h - 2) * 64
        x = _pick_half(low, h % 2, field[h // 2].astype(BF), zero)
        field[h] += _nt(x, wide[row : row + 128, :])
    for s in range(32):
        x = field[32 + s]
        top, bottom = x[:8], x[8:]
        out_ref[2 * s] = jnp.where(low8, top, _roll(bottom)).astype(BF)
        out_ref[2 * s + 1] = jnp.where(low8, _roll(top), bottom).astype(BF)


def near_kernel(
    me_ref, ids_ref, inner_hbm, own_hbm, own2_hbm, outer_hbm, blocks_hbm, mine_out, other_out, halo, own, blocks_ref, leaves, sems
):
    copies = _fetch(
        sems,
        (own_hbm, own.at[0:R]),
        (own2_hbm, own.at[R:]),
        (inner_hbm.at[64:128], halo.at[0]),
        (outer_hbm.at[64:128], halo.at[1]),
        *_chunks(blocks_hbm, blocks_ref, 2),
    )
    for copy in copies[:4]:
        copy.wait()
    core = me_ref[0] % 2
    for s in range(32):
        for part in range(3):
            if part == 1:
                z = own[:, 128 * s : 128 * s + 128]
            else:
                side = 1 - core if part == 0 else core
                z = jnp.concatenate([halo[side, s], halo[side, 32 + s]], axis=0)
            e = 64 * part + 2 * s
            leaves[e] = z[:, :64]
            leaves[e + 1] = z[:, 64:]
    start = (me_ref[0] - 1) * 64
    for p in range(32):
        if p % (32 // 2) == 0:
            copies[4 + p // (32 // 2)].wait()
        parts = []
        for i in (2 * p, 2 * p + 1):
            total = _nt(leaves[ids_ref[0, i] - start], blocks_ref[i, 0])
            for j in range(1, 4):
                total += _nt(leaves[ids_ref[j, i] - start], blocks_ref[i, j])
            parts.append(total)
        pair = jnp.concatenate(parts, axis=1)
        mine_out[:, 128 * p : 128 * p + 128] = pair[:R]
        other_out[:, 128 * p : 128 * p + 128] = pair[R:].astype(BF)


def field_kernel(me_ref, ids_ref, inner_hbm, own_hbm, outer_hbm, raw_hbm, out_ref, raw_ref, wide, seen, coef, sems):
    copies = _fetch(
        sems,
        (inner_hbm.at[0:64], seen.at[0]),
        (own_hbm.at[0:64], seen.at[1]),
        (outer_hbm.at[0:64], seen.at[2]),
        *[(raw_hbm.at[:, 32 * i : 32 * i + 32], raw_ref.at[:, 32 * i : 32 * i + 32]) for i in range(2)],
    )
    low = _low(R)
    core = me_ref[0] % 2
    for copy in copies[:3]:
        copy.wait()
    for part in range(3):
        side = (2 - 2 * core, 1, 2 * core)[part]
        for s in range(64):
            x = seen[side, s]
            y = jnp.concatenate([x[:, 64:], x[:, :64]], axis=1)
            coef[part * NODES + 2 * s] = jnp.where(low, x, y)
            coef[part * NODES + 2 * s + 1] = jnp.where(low, y, x)
    eye = _eye(raw_ref.shape[3])
    for m in range(64):
        if m % 32 == 0:
            copies[3 + m // 32].wait()
        for k in range(2):
            both = jnp.concatenate([raw_ref[k, m], raw_ref[k + 2, m]], axis=0)
            wide[pl.ds(k * 64 + m, NODES, stride=PITCH_FIELD), :] = _nt(eye, both)
    before = me_ref[0] - 1

    def source(k, t):
        level = next(i for i in range(7) if t < FIRST[i] + SIZES[i])
        e = ids_ref[k, t] - before * SIZES[level]
        part = lax.shift_right_logical(e, 6 - level)
        return coef[part * NODES + (e & (SIZES[level] - 1)) + FIRST[level]]

    def node(t):
        a = jnp.where(low, source(0, t), source(1, t))
        b = jnp.where(low, source(2, t), source(3, t))
        y = _nn(jnp.concatenate([a, b], axis=0), wide[PITCH_FIELD * t : PITCH_FIELD * t + 128, :].astype(BF))
        return y[:R], y[R:]

    for s in range(63):
        a0, b0 = node(2 * s)
        a1, b1 = node(2 * s + 1)
        out_ref[s] = jnp.where(low, a0, b1) + _roll(jnp.where(low, a1, b0))
    a0, b0 = node(126)
    out_ref[63] = a0 + _roll(b0)


def down_kernel(
    me_ref, mine_ref, other_ref, field_ref, wide_hbm, basis_hbm, near_ref, near2_ref, out_ref, down, wide_ref, basis_ref, sems
):
    rows = (NODES * 64, 96 * 64, 64 * 64, 32 * 64, 0)
    spans = [(b, a) for a, b in zip(rows, rows[1:])]
    copies = _fetch(
        sems,
        *[(wide_hbm.at[a:b], wide_ref.at[a:b]) for a, b in spans],
        *_chunks(basis_hbm, basis_ref, 2),
    )
    core = me_ref[0] % 2
    low = _low(R)
    zero = jnp.zeros((R, 128), BF)
    first = jnp.where(core == 0, mine_ref[...], other_ref[...])
    second = jnp.where(core == 0, other_ref[...], mine_ref[...])
    upper = jnp.concatenate([first, _roll(first), second, _roll(second)], axis=0)
    upper = jnp.where(low, upper, 0.0).astype(BF)
    copies[0].wait()
    root = field_ref[63][:, :64] + _nt(upper, wide_ref[126 * 64 : 127 * 64, :])
    down[63] = jnp.concatenate([root, root], axis=1).astype(BF)
    for level in range(5, -1, -1):
        for q in range(SIZES[level + 1]):
            if level == 1 and q == 0:
                copies[1].wait()
            if level == 0 and q % 16 == 0:
                copies[3 - q // 16].wait()
            row = (FIRST[level] + 2 * q) * 64
            x = _pick_half(low, q % 2, down[SLOT[level + 1] + q // 2], zero)
            s = SLOT[level] + q
            down[s] = (field_ref[s] + _nt(x, wide_ref[row : row + 128, :])).astype(BF)
    for p in range(32):
        if p % 16 == 0:
            copies[4 + p // 16].wait()
        d = down[p]
        both = jnp.concatenate([d[:, :64], d[:, 64:]], axis=0)
        y = _nt(both, basis_ref[2 * p : 2 * p + 2].reshape(128, 64))
        lanes = slice(128 * p, 128 * p + 128)
        total = jnp.where(low, y[:R], y[R:]) + near_ref[:, lanes] + near2_ref[:, lanes].astype(F32)
        out_ref[:, lanes] = total.astype(BF)


def _call(body, name, outs, ins, scratch, limit, micros, out_specs=None):
    vm = pl.BlockSpec(memory_space=pltpu.VMEM)
    if out_specs is None:
        out_specs = (vm,) * len(outs) if isinstance(outs, tuple) else vm
    return pl.pallas_call(
        body,
        out_shape=outs,
        in_specs=ins,
        out_specs=out_specs,
        scratch_shapes=scratch,
        compiler_params=pltpu.CompilerParams(vmem_limit_bytes=limit * MIB),
        cost_estimate=pl.CostEstimate(
            flops=int(micros * 1.0e9), bytes_accessed=int(micros * 3.0e6), transcendentals=0
        ),
        name=name,
    )


def shards(
    vectors,
    leaf_basis,
    local_transfer,
    coupling,
    coupling_source,
    top_transfer,
    top_coupling,
    top_target,
    top_source,
    near_blocks,
    near_source,
):
    n_leaf = lax.axis_size("leaf")
    me = lax.axis_index("leaf").astype(jnp.int32).reshape(1)
    vm = pl.BlockSpec(memory_space=pltpu.VMEM)
    sm = pl.BlockSpec(memory_space=pltpu.SMEM)
    S = jax.ShapeDtypeStruct
    pair = [(i, i ^ 1) for i in range(n_leaf)]
    across = [(i, i + 1) for i in range(1, n_leaf - 1, 2)]
    across += [(j, i) for i, j in across]
    swap = [(0, 1), (1, 0)]
    groups = [[2 * i + c for i in range(n_leaf // 2)] for c in range(2)]

    vectors2 = lax.ppermute(vectors, "rhs", swap)
    top_target2 = lax.ppermute(top_target, "leaf", pair)
    top_source2 = lax.ppermute(top_source, "leaf", pair)
    top_coupling2 = lax.ppermute(top_coupling, "leaf", pair)

    hbm = pl.BlockSpec(memory_space=pltpu.HBM)
    any_ = pl.BlockSpec(memory_space=pl.ANY)
    dma = pltpu.SemaphoreType.DMA
    V = pltpu.VMEM
    raw = jnp.transpose(local_transfer, (1, 2, 0))
    msg, root, wide = _call(
        up_kernel,
        "up",
        (S((128, R, 128), BF), S((R, 128), F32), S((NODES * 64, 128), BF)),
        [hbm, hbm, hbm],
        [
            V(vectors.shape, BF),
            V(leaf_basis.shape, BF),
            V(raw.shape, BF),
            V((NODES * PITCH, 128), F32),
            V((NODES * 64, 128), BF),
            dma((6,)),
            dma((1,)),
        ],
        60,
        4,
        (vm, vm, hbm),
    )(vectors, leaf_basis, raw)

    root2 = lax.ppermute(root, "leaf", pair)
    send = _call(pack_kernel, "pack", S((n_leaf // 2, 8, 128), BF), [sm, vm, vm, any_, any_, any_], [], 4, 0.5)(
        me, root, root2, top_coupling2, top_target2, top_source2
    )
    gathered = lax.all_to_all(send, "leaf", 0, 0, tiled=True, axis_index_groups=groups)

    raw = jnp.transpose(top_transfer, (1, 2, 0))
    wide_top, done = _call(
        top_kernel,
        "top",
        (S((NODES * 64, 128), BF), S((8, 128), F32)),
        [hbm, any_],
        [
            V(raw.shape, BF),
            V((NODES * PITCH, 128), F32),
            V((NODES * 64, 128), BF),
            dma((1,)),
            dma((1,)),
        ],
        57,
        4,
        (hbm, vm),
    )(raw, send)

    msg = pl.pallas_call(
        bundle_kernel,
        grid=(1,),
        out_shape=S((128, R, 128), BF),
        in_specs=[any_, vm, any_, any_],
        out_specs=pl.BlockSpec((32, R, 128), lambda i: (3, 0, 0)),
        input_output_aliases={0: 0},
        compiler_params=pltpu.CompilerParams(vmem_limit_bytes=4 * MIB),
        cost_estimate=pl.CostEstimate(flops=0, bytes_accessed=1000000, transcendentals=0),
        name="bundle",
    )(msg, vectors2, done, gathered)
    inner = lax.ppermute(msg, "leaf", pair)
    outer = lax.ppermute(msg, "leaf", across)
    partial = _call(
        upper_kernel,
        "upper",
        S((n_leaf // 2, 8, 128), BF),
        [sm, sm, sm, sm, vm, hbm, any_, any_],
        [
            V((NODES * 64, 128), BF),
            V((8, 64, 64), BF),
            V((64, 16, 128), BF),
            V((64, 16, 128), F32),
            dma((3,)),
        ],
        57,
        6,
    )(top_target, top_source, top_target2, top_source2, gathered, wide_top, top_coupling, top_coupling2)
    parts = lax.all_to_all(partial, "leaf", 0, 0, tiled=True, axis_index_groups=groups)

    near_mine, near_send = _call(
        near_kernel,
        "near",
        (S((R, 4096), F32), S((R, 4096), BF)),
        [sm, sm, any_, any_, any_, any_, hbm],
        [
            V((2, 64, R, 128), BF),
            V((2 * R, 4096), BF),
            V(near_blocks.shape, BF),
            V((192, 64, 64), BF),
            dma((12,)),
        ],
        52,
        5,
    )(me, near_source.T, inner, vectors, vectors2, outer, near_blocks)
    near_other = lax.ppermute(near_send, "rhs", swap)
    parts, near_mine = lax.optimization_barrier((parts, near_mine))
    mine = _call(sum_kernel, "total", S((8, 128), F32), [vm], [], 4, 0.5)(parts)
    other = lax.ppermute(mine, "leaf", pair)

    raw = jnp.transpose(coupling, (1, 2, 3, 0))
    fields = _call(
        field_kernel,
        "field",
        S((64, R, 128), F32),
        [sm, sm, any_, any_, any_, hbm],
        [
            V(raw.shape, BF),
            V((NODES * PITCH_FIELD, 128), F32),
            V((3, 64, R, 128), BF),
            V((3 * NODES, R, 128), BF),
            dma((5,)),
        ],
        52,
        8,
    )(me, coupling_source.T, inner, msg, outer, raw)

    return _call(
        down_kernel,
        "down",
        S((R, 4096), BF),
        [sm, vm, vm, vm, hbm, hbm, vm, vm],
        [V((64, R, 128), BF), V((NODES * 64, 128), BF), V(leaf_basis.shape, BF), dma((6,))],
        10,
        4,
    )(me, mine, other, fields, wide, leaf_basis, near_mine, near_other)


def solution(mesh):
    placed = (
        P("rhs", "leaf"),
        P("leaf", None, None),
        P("leaf", None, None),
        P("leaf", None, None, None),
        P("leaf", None),
        P(),
        P("leaf", None, None),
        P("leaf"),
        P("leaf"),
        P("leaf", "rhs", None, None),
        P("leaf", "rhs"),
    )
    return jax.shard_map(
        shards, mesh=mesh, in_specs=placed, out_specs=P("rhs", "leaf"), check_vma=False
    )
```

```python
import jax
import jax.numpy as jnp
from jax import lax
from jax.experimental import pallas as pl
from jax.experimental.pallas import tpu as pltpu
from jax.sharding import PartitionSpec as P

BF = jnp.bfloat16
F32 = jnp.float32
MIB = 1024 * 1024

NODES = 128
SIZES = (64, 32, 16, 8, 4, 2, 1)
FIRST = (0, 64, 96, 112, 120, 124, 126)
SLOT = (0, 32, 48, 56, 60, 62, 63)
R = 32


def _nn(a, b):
    return lax.dot_general(a, b, (((1,), (0,)), ((), ())), preferred_element_type=F32)


def _nt(a, b):
    return lax.dot_general(a, b, (((1,), (1,)), ((), ())), preferred_element_type=F32)


def _low(rows):
    return lax.broadcasted_iota(jnp.int32, (rows, 128), 1) < 64


def _pick_half(low, half, x, zero):
    return jnp.where(low == (half == 0), x, zero)


def _roll(x):
    return pltpu.roll(x, 64, 1)


PITCH = 72
PITCH_FIELD = 136


def _fetch(sems, *moves):
    copies = [pltpu.make_async_copy(src, dst, sems.at[i]) for i, (src, dst) in enumerate(moves)]
    for copy in copies:
        copy.start()
    return copies


def _chunks(src, dst, parts):
    size = src.shape[0] // parts
    return [
        (src.at[i * size : (i + 1) * size], dst.at[i * size : (i + 1) * size]) for i in range(parts)
    ]


def _unstack(raw_ref, wide, copy):
    copy.wait()
    for k in range(64):
        block = raw_ref[k].astype(F32)
        both = jnp.concatenate([block, block], axis=0)
        wide[pl.ds(k, raw_ref.shape[2], stride=PITCH), :] = both.T


def _narrow(wide, out_ref, nodes):
    for t in range(nodes):
        out_ref[64 * t : 64 * t + 64, :] = wide[PITCH * t : PITCH * t + 64, :].astype(BF)


def up_kernel(
    v_hbm, basis_hbm, raw_hbm, msg_hbm, root_ref, wide_hbm, v_ref, basis_ref, raw_ref, msg_ref, wide, wide_ref, sems, out_sems
):
    copies = _fetch(sems, (raw_hbm, raw_ref), (v_hbm, v_ref), (basis_hbm, basis_ref))
    low = _low(R)
    zero = jnp.zeros((R, 128), BF)
    _unstack(raw_ref, wide, copies[0])
    _narrow(wide, wide_ref, raw_ref.shape[2])
    out = _fetch(out_sems, (wide_ref, wide_hbm))
    copies[1].wait()
    copies[2].wait()
    for p in range(32):
        v = v_ref[:, 128 * p : 128 * p + 128]
        msg_ref[64 + p] = v
        both = jnp.concatenate([jnp.where(low, v, zero), jnp.where(low, zero, v)], axis=0)
        y = _nn(both, basis_ref[2 * p : 2 * p + 2].reshape(128, 64))
        msg_ref[p] = jnp.concatenate([y[:R], y[R:]], axis=1).astype(BF)
    out += _fetch(
        out_sems.at[1:3], (msg_ref.at[0:32], msg_hbm.at[0:32]), (msg_ref.at[64:96], msg_hbm.at[64:96])
    )
    for level in range(1, 7):
        for s in range(max(1, SIZES[level] // 2)):
            parts = []
            for q in (2 * s, 2 * s + 1)[: min(2, SIZES[level])]:
                row = (FIRST[level - 1] + 2 * q) * 64
                parts.append(_nn(msg_ref[SLOT[level - 1] + q], wide_ref[row : row + 128, :]))
            value = parts[0] if len(parts) == 1 else jnp.where(low, parts[0], parts[1])
            msg_ref[SLOT[level] + s] = value.astype(BF)
    out += _fetch(out_sems.at[3:4], (msg_ref.at[32:64], msg_hbm.at[32:64]))
    root_ref[...] = _nn(msg_ref[63][:, :64], wide_ref[126 * 64 : 127 * 64, :])
    for copy in out:
        copy.wait()


def pack_kernel(me_ref, mine_ref, other_ref, out_ref):
    core = me_ref[0] & 1
    total = mine_ref[...] + other_ref[...]
    half = jnp.where(core == 0, total[:16], total[16:])
    packed = jnp.where(_low(8), half[:8], half[8:]).astype(BF)
    out_ref[...] = jnp.broadcast_to(packed[None], out_ref.shape)


def sum_kernel(parts_ref, out_ref):
    out_ref[...] = jnp.sum(parts_ref[...].astype(F32), axis=0)


def bundle_kernel(msg_ref, other_ref, gathered_ref, out_ref):
    for s in range(32):
        out_ref[s] = other_ref[:, 128 * s : 128 * s + 128]


def top_kernel(raw_hbm, msg_hbm, send_hbm, block_hbm, target_hbm, source_hbm, wide_hbm, msg_out, raw_ref, wide, wide_ref, sems, out_sems):
    copies = _fetch(sems, (raw_hbm, raw_ref))
    _unstack(raw_ref, wide, copies[0])
    _narrow(wide, wide_ref, raw_ref.shape[2])
    out = _fetch(out_sems, (wide_ref, wide_hbm))
    out[0].wait()


def upper_kernel(
    target_ref, source_ref, target2_ref, source2_ref, gathered_ref, wide_hbm, blocks_hbm, blocks2_hbm, out_ref, wide, blocks_ref, coef, field, sems
):
    copies = _fetch(
        sems,
        (wide_hbm.at[62 * 64 :], wide.at[62 * 64 :]),
        (wide_hbm.at[: 62 * 64], wide.at[: 62 * 64]),
        (blocks_hbm, blocks_ref.at[0:4]),
        (blocks2_hbm, blocks_ref.at[4:8]),
    )
    low8, low = _low(8), _low(16)
    zero = jnp.zeros((16, 128), BF)
    zero32 = jnp.zeros((16, 128), F32)
    for s in range(32):
        a, b = gathered_ref[63 - 2 * s].astype(F32), gathered_ref[62 - 2 * s].astype(F32)
        top = jnp.where(low8, a, _roll(b))
        bottom = jnp.where(low8, _roll(a), b)
        coef[32 + s] = jnp.concatenate([top, bottom], axis=0).astype(BF)
    field[...] = jnp.zeros_like(field)
    copies[0].wait()
    size = 32
    while size >= 2:
        if size == 16:
            copies[1].wait()
        for s in range(size // 2, size):
            parts = []
            for h in (2 * s, 2 * s + 1):
                row = (2 * h - 2) * 64
                parts.append(_nn(coef[h], wide[row : row + 128, :]))
            coef[s] = jnp.where(low, parts[0], parts[1]).astype(BF)
        size //= 2
    copies[2].wait()
    copies[3].wait()
    for b in range(8):
        target = target_ref[b] if b < 4 else target2_ref[b - 4]
        source = source_ref[b] if b < 4 else source2_ref[b - 4]
        block = blocks_ref[b]
        block = jnp.concatenate([block, block], axis=0)
        block = jnp.concatenate([block, block], axis=1)
        x = _pick_half(low, source & 1, coef[source >> 1], zero)
        field[target >> 1] += _pick_half(low, target & 1, _nn(x, block), zero32)
    for h in range(2, 64):
        row = (2 * h - 2) * 64
        x = _pick_half(low, h % 2, field[h // 2].astype(BF), zero)
        field[h] += _nt(x, wide[row : row + 128, :])
    for s in range(32):
        x = field[32 + s]
        top, bottom = x[:8], x[8:]
        out_ref[63 - 2 * s] = jnp.where(low8, top, _roll(bottom)).astype(BF)
        out_ref[62 - 2 * s] = jnp.where(low8, _roll(top), bottom).astype(BF)


def near_kernel(
    me_ref, ids_ref, inner_hbm, own_hbm, own2_hbm, outer_hbm, blocks_hbm, mine_out, other_out, halo, own, blocks_ref, leaves, sems
):
    copies = _fetch(
        sems,
        (own_hbm, own.at[0:R]),
        (own2_hbm, own.at[R:]),
        (inner_hbm.at[64:128], halo.at[0]),
        (outer_hbm.at[64:128], halo.at[1]),
        *_chunks(blocks_hbm, blocks_ref, 2),
    )
    for copy in copies[:4]:
        copy.wait()
    core = me_ref[0] & 1
    for s in range(32):
        for part in range(3):
            if part == 1:
                z = own[:, 128 * s : 128 * s + 128]
            else:
                side = 1 - core if part == 0 else core
                z = jnp.concatenate([halo[side, s], halo[side, 32 + s]], axis=0)
            e = 64 * part + 2 * s
            leaves[e] = z[:, :64]
            leaves[e + 1] = z[:, 64:]
    start = (me_ref[0] - 1) * 64
    for p in range(32):
        if p % (32 // 2) == 0:
            copies[4 + p // (32 // 2)].wait()
        parts = []
        for i in (2 * p, 2 * p + 1):
            total = _nt(leaves[ids_ref[0, i] - start], blocks_ref[i, 0])
            for j in range(1, 4):
                total += _nt(leaves[ids_ref[j, i] - start], blocks_ref[i, j])
            parts.append(total)
        pair = jnp.concatenate(parts, axis=1)
        mine_out[:, 128 * p : 128 * p + 128] = pair[:R]
        other_out[:, 128 * p : 128 * p + 128] = pair[R:].astype(BF)


def field_kernel(me_ref, ids_ref, inner_hbm, own_hbm, outer_hbm, raw_hbm, out_ref, raw_ref, wide, seen, coef, sems):
    copies = _fetch(
        sems,
        (inner_hbm.at[0:64], seen.at[0]),
        (own_hbm.at[0:64], seen.at[1]),
        (outer_hbm.at[0:64], seen.at[2]),
        *[(raw_hbm.at[:, 32 * i : 32 * i + 32], raw_ref.at[:, 32 * i : 32 * i + 32]) for i in range(2)],
    )
    low = _low(R)
    core = me_ref[0] & 1
    for copy in copies[:3]:
        copy.wait()
    for part in range(3):
        side = (2 - 2 * core, 1, 2 * core)[part]
        for s in range(64):
            x = seen[side, s]
            y = jnp.concatenate([x[:, 64:], x[:, :64]], axis=1)
            coef[part * NODES + 2 * s] = jnp.where(low, x, y)
            coef[part * NODES + 2 * s + 1] = jnp.where(low, y, x)
    for m in range(64):
        if m % 32 == 0:
            copies[3 + m // 32].wait()
        for k in range(2):
            both = jnp.concatenate([raw_ref[k, m], raw_ref[k + 2, m]], axis=0).astype(F32)
            wide[pl.ds(k * 64 + m, raw_ref.shape[3], stride=PITCH_FIELD), :] = both.T
    before = me_ref[0] - 1

    def source(k, t):
        level = next(i for i in range(7) if t < FIRST[i] + SIZES[i])
        e = ids_ref[k, t] - before * SIZES[level]
        part = lax.shift_right_logical(e, 6 - level)
        return coef[part * NODES + (e & (SIZES[level] - 1)) + FIRST[level]]

    def node(t):
        a = jnp.where(low, source(0, t), source(1, t))
        b = jnp.where(low, source(2, t), source(3, t))
        y = _nn(jnp.concatenate([a, b], axis=0), wide[PITCH_FIELD * t : PITCH_FIELD * t + 128, :].astype(BF))
        return y[:R], y[R:]

    for s in range(63):
        a0, b0 = node(2 * s)
        a1, b1 = node(2 * s + 1)
        out_ref[s] = jnp.where(low, a0, b1) + _roll(jnp.where(low, a1, b0))
    a0, b0 = node(126)
    out_ref[63] = a0 + _roll(b0)


def down_kernel(me_ref, mine_ref, other_ref, field_ref, wide_ref, basis_ref, near_ref, near2_ref, out_ref, down):
    core = me_ref[0] & 1
    low = _low(R)
    zero = jnp.zeros((R, 128), BF)
    first = jnp.where(core == 0, mine_ref[...], other_ref[...])
    second = jnp.where(core == 0, other_ref[...], mine_ref[...])
    upper = jnp.concatenate([first, _roll(first), second, _roll(second)], axis=0)
    upper = jnp.where(low, upper, 0.0).astype(BF)
    root = field_ref[63][:, :64] + _nt(upper, wide_ref[126 * 64 : 127 * 64, :])
    down[63] = jnp.concatenate([root, root], axis=1).astype(BF)
    for level in range(5, -1, -1):
        for q in range(SIZES[level + 1]):
            row = (FIRST[level] + 2 * q) * 64
            x = _pick_half(low, q % 2, down[SLOT[level + 1] + q // 2], zero)
            s = SLOT[level] + q
            down[s] = (field_ref[s] + _nt(x, wide_ref[row : row + 128, :])).astype(BF)
    for p in range(32):
        d = down[p]
        both = jnp.concatenate([d[:, :64], d[:, 64:]], axis=0)
        y = _nt(both, basis_ref[2 * p : 2 * p + 2].reshape(128, 64))
        lanes = slice(128 * p, 128 * p + 128)
        total = jnp.where(low, y[:R], y[R:]) + near_ref[:, lanes] + near2_ref[:, lanes].astype(F32)
        out_ref[:, lanes] = total.astype(BF)


def _call(body, name, outs, ins, scratch, limit, micros, out_specs=None, aliases={}):
    vm = pl.BlockSpec(memory_space=pltpu.VMEM)
    if out_specs is None:
        out_specs = (vm,) * len(outs) if isinstance(outs, tuple) else vm
    return pl.pallas_call(
        body,
        out_shape=outs,
        in_specs=ins,
        out_specs=out_specs,
        scratch_shapes=scratch,
        input_output_aliases=aliases,
        compiler_params=pltpu.CompilerParams(vmem_limit_bytes=limit * MIB),
        cost_estimate=pl.CostEstimate(
            flops=int(micros * 1.0e9), bytes_accessed=int(micros * 3.0e6), transcendentals=0
        ),
        name=name,
    )


def shards(
    vectors,
    leaf_basis,
    local_transfer,
    coupling,
    coupling_source,
    top_transfer,
    top_coupling,
    top_target,
    top_source,
    near_blocks,
    near_source,
):
    n_leaf = lax.axis_size("leaf")
    me = lax.axis_index("leaf").astype(jnp.int32).reshape(1)
    vm = pl.BlockSpec(memory_space=pltpu.VMEM)
    sm = pl.BlockSpec(memory_space=pltpu.SMEM)
    S = jax.ShapeDtypeStruct
    pair = [(i, i ^ 1) for i in range(n_leaf)]
    across = [(i, i + 1) for i in range(1, n_leaf - 1, 2)]
    across += [(j, i) for i, j in across]
    swap = [(0, 1), (1, 0)]
    groups = [[2 * i + c for i in reversed(range(n_leaf // 2))] for c in range(2)]

    hbm = pl.BlockSpec(memory_space=pltpu.HBM)
    any_ = pl.BlockSpec(memory_space=pl.ANY)
    dma = pltpu.SemaphoreType.DMA
    V = pltpu.VMEM
    raw = jnp.transpose(local_transfer, (1, 2, 0))
    msg, root, wide = _call(
        up_kernel,
        "up",
        (S((128, R, 128), BF), S((R, 128), F32), S((NODES * 64, 128), BF)),
        [hbm, hbm, hbm],
        [
            V(vectors.shape, BF),
            V(leaf_basis.shape, BF),
            V(raw.shape, BF),
            V((96, R, 128), BF),
            V((NODES * PITCH, 128), F32),
            V((NODES * 64, 128), BF),
            dma((3,)),
            dma((4,)),
        ],
        59,
        4,
        (hbm, vm, hbm),
    )(vectors, leaf_basis, raw)

    root2 = lax.ppermute(root, "leaf", pair)
    send = _call(pack_kernel, "pack", S((n_leaf // 2, 8, 128), BF), [sm, vm, vm], [], 4, 0.5)(
        me, root, root2
    )
    gathered = lax.all_to_all(send, "leaf", 0, 0, tiled=True, axis_index_groups=groups)
    vectors2 = lax.ppermute(vectors, "rhs", swap)
    block, target, source, _ = lax.optimization_barrier(
        (top_coupling, top_target, top_source, send)
    )
    top_coupling2 = lax.ppermute(block, "leaf", pair)
    top_target2 = lax.ppermute(target, "leaf", pair)
    top_source2 = lax.ppermute(source, "leaf", pair)

    raw = jnp.transpose(top_transfer, (1, 2, 0))
    wide_top, msg = _call(
        top_kernel,
        "top",
        (S((NODES * 64, 128), BF), S((128, R, 128), BF)),
        [hbm] + [any_] * 5,
        [
            V(raw.shape, BF),
            V((NODES * PITCH, 128), F32),
            V((NODES * 64, 128), BF),
            dma((1,)),
            dma((1,)),
        ],
        57,
        4,
        (hbm, any_),
        {1: 1},
    )(raw, msg, send, top_coupling2, top_target2, top_source2)

    msg = pl.pallas_call(
        bundle_kernel,
        grid=(1,),
        out_shape=S((128, R, 128), BF),
        in_specs=[any_, vm, any_],
        out_specs=pl.BlockSpec((32, R, 128), lambda i: (3, 0, 0)),
        input_output_aliases={0: 0},
        compiler_params=pltpu.CompilerParams(vmem_limit_bytes=4 * MIB),
        cost_estimate=pl.CostEstimate(flops=0, bytes_accessed=1000000, transcendentals=0),
        name="bundle",
    )(msg, vectors2, gathered)
    inner = lax.ppermute(msg, "leaf", pair)
    outer = lax.ppermute(msg, "leaf", across)
    partial = _call(
        upper_kernel,
        "upper",
        S((n_leaf // 2, 8, 128), BF),
        [sm, sm, sm, sm, vm, hbm, any_, any_],
        [
            V((NODES * 64, 128), BF),
            V((8, 64, 64), BF),
            V((64, 16, 128), BF),
            V((64, 16, 128), F32),
            dma((4,)),
        ],
        57,
        6,
    )(top_target, top_source, top_target2, top_source2, gathered, wide_top, top_coupling, top_coupling2)
    parts = lax.all_to_all(partial, "leaf", 0, 0, tiled=True, axis_index_groups=groups)

    near_mine, near_send = _call(
        near_kernel,
        "near",
        (S((R, 4096), F32), S((R, 4096), BF)),
        [sm, sm, any_, any_, any_, any_, hbm],
        [
            V((2, 64, R, 128), BF),
            V((2 * R, 4096), BF),
            V(near_blocks.shape, BF),
            V((192, 64, 64), BF),
            dma((12,)),
        ],
        49,
        5,
    )(me, near_source.T, inner, vectors, vectors2, outer, near_blocks)
    near_other = lax.ppermute(near_send, "rhs", swap)
    parts, near_mine = lax.optimization_barrier((parts, near_mine))
    mine = _call(sum_kernel, "total", S((8, 128), F32), [vm], [], 4, 0.5)(parts)
    other = lax.ppermute(mine, "leaf", pair)

    raw = jnp.transpose(coupling, (1, 2, 3, 0))
    fields = _call(
        field_kernel,
        "field",
        S((64, R, 128), F32),
        [sm, sm, any_, any_, any_, hbm],
        [
            V(raw.shape, BF),
            V((NODES * PITCH_FIELD, 128), F32),
            V((3, 64, R, 128), BF),
            V((3 * NODES, R, 128), BF),
            dma((5,)),
        ],
        49,
        2,
    )(me, coupling_source.T, inner, msg, outer, raw)

    return _call(
        down_kernel,
        "down",
        S((R, 4096), BF),
        [sm] + [vm] * 7,
        [V((64, R, 128), BF)],
        10,
        4,
    )(me, mine, other, fields, wide, leaf_basis, near_mine, near_other)


def solution(mesh):
    placed = (
        P("rhs", "leaf"),
        P("leaf", None, None),
        P("leaf", None, None),
        P("leaf", None, None, None),
        P("leaf", None),
        P(),
        P("leaf", None, None),
        P("leaf"),
        P("leaf"),
        P("leaf", "rhs", None, None),
        P("leaf", "rhs"),
    )
    return jax.shard_map(
        shards, mesh=mesh, in_specs=placed, out_specs=P("rhs", "leaf"), check_vma=False
    )
```

```python
import jax
import jax.numpy as jnp
from jax import lax
from jax.experimental import pallas as pl
from jax.experimental.pallas import tpu as pltpu
from jax.sharding import PartitionSpec as P

BF = jnp.bfloat16
F32 = jnp.float32
MIB = 1024 * 1024

NODES = 128
SIZES = (64, 32, 16, 8, 4, 2, 1)
FIRST = (0, 64, 96, 112, 120, 124, 126)
SLOT = (0, 32, 48, 56, 60, 62, 63)
R = 32


def _nn(a, b):
    return lax.dot_general(a, b, (((1,), (0,)), ((), ())), preferred_element_type=F32)


def _nt(a, b):
    return lax.dot_general(a, b, (((1,), (1,)), ((), ())), preferred_element_type=F32)


def _low(rows):
    return lax.broadcasted_iota(jnp.int32, (rows, 128), 1) < 64


def _pick_half(low, half, x, zero):
    return jnp.where(low == (half == 0), x, zero)


def _roll(x):
    return pltpu.roll(x, 64, 1)


PITCH = 72
PITCH_FIELD = 136


def _fetch(sems, *moves):
    copies = [pltpu.make_async_copy(src, dst, sems.at[i]) for i, (src, dst) in enumerate(moves)]
    for copy in copies:
        copy.start()
    return copies


def _chunks(src, dst, parts):
    size = src.shape[0] // parts
    return [
        (src.at[i * size : (i + 1) * size], dst.at[i * size : (i + 1) * size]) for i in range(parts)
    ]


def _unstack(raw_ref, wide, copies):
    for k in range(64):
        if k % 32 == 0:
            copies[k // 32].wait()
        block = raw_ref[k].astype(F32)
        both = jnp.concatenate([block, block], axis=0)
        wide[pl.ds(k, raw_ref.shape[2], stride=PITCH), :] = both.T


def _narrow(wide, out_ref, nodes):
    for t in range(nodes):
        out_ref[64 * t : 64 * t + 64, :] = wide[PITCH * t : PITCH * t + 64, :].astype(BF)


def up_kernel(
    v_hbm, basis_hbm, raw_hbm, msg_hbm, root_ref, wide_hbm, v_ref, basis_ref, raw_ref, msg_ref, wide, wide_ref, sems, out_sems
):
    copies = _fetch(sems, *_chunks(raw_hbm, raw_ref, 2), (v_hbm, v_ref), (basis_hbm, basis_ref))
    low = _low(R)
    zero = jnp.zeros((R, 128), BF)
    _unstack(raw_ref, wide, copies)
    _narrow(wide, wide_ref, raw_ref.shape[2])
    out = _fetch(out_sems, (wide_ref, wide_hbm))
    copies[2].wait()
    copies[3].wait()
    for p in range(32):
        v = v_ref[:, 128 * p : 128 * p + 128]
        msg_ref[64 + p] = v
        both = jnp.concatenate([jnp.where(low, v, zero), jnp.where(low, zero, v)], axis=0)
        y = _nn(both, basis_ref[2 * p : 2 * p + 2].reshape(128, 64))
        msg_ref[p] = jnp.concatenate([y[:R], y[R:]], axis=1).astype(BF)
    out += _fetch(
        out_sems.at[1:3], (msg_ref.at[0:32], msg_hbm.at[0:32]), (msg_ref.at[64:96], msg_hbm.at[64:96])
    )
    for level in range(1, 7):
        for s in range(max(1, SIZES[level] // 2)):
            parts = []
            for q in (2 * s, 2 * s + 1)[: min(2, SIZES[level])]:
                row = (FIRST[level - 1] + 2 * q) * 64
                parts.append(_nn(msg_ref[SLOT[level - 1] + q], wide_ref[row : row + 128, :]))
            value = parts[0] if len(parts) == 1 else jnp.where(low, parts[0], parts[1])
            msg_ref[SLOT[level] + s] = value.astype(BF)
    out += _fetch(out_sems.at[3:4], (msg_ref.at[32:64], msg_hbm.at[32:64]))
    root_ref[...] = _nn(msg_ref[63][:, :64], wide_ref[126 * 64 : 127 * 64, :])
    for copy in out:
        copy.wait()


def pack_kernel(me_ref, mine_ref, other_ref, out_ref):
    core = me_ref[0] & 1
    total = mine_ref[...] + other_ref[...]
    half = jnp.where(core == 0, total[:16], total[16:])
    packed = jnp.where(_low(8), half[:8], half[8:]).astype(BF)
    out_ref[...] = jnp.broadcast_to(packed[None], out_ref.shape)


def sum_kernel(parts_ref, out_ref):
    out_ref[...] = jnp.sum(parts_ref[...].astype(F32), axis=0)


def bundle_kernel(msg_ref, other_ref, gathered_ref, out_ref):
    for s in range(32):
        out_ref[s] = other_ref[:, 128 * s : 128 * s + 128]


def top_kernel(raw_hbm, msg_hbm, send_hbm, block_hbm, target_hbm, source_hbm, wide_hbm, msg_out, raw_ref, wide, wide_ref, sems, out_sems):
    copies = _fetch(sems, *_chunks(raw_hbm, raw_ref, 2))
    _unstack(raw_ref, wide, copies)
    _narrow(wide, wide_ref, raw_ref.shape[2])
    out = _fetch(out_sems, (wide_ref, wide_hbm))
    out[0].wait()


def upper_kernel(
    target_ref, source_ref, target2_ref, source2_ref, gathered_ref, wide_hbm, blocks_hbm, blocks2_hbm, out_ref, wide, blocks_ref, coef, field, sems
):
    copies = _fetch(
        sems,
        (wide_hbm.at[62 * 64 :], wide.at[62 * 64 :]),
        (wide_hbm.at[: 62 * 64], wide.at[: 62 * 64]),
        (blocks_hbm, blocks_ref.at[0:4]),
        (blocks2_hbm, blocks_ref.at[4:8]),
    )
    low8, low = _low(8), _low(16)
    zero = jnp.zeros((16, 128), BF)
    zero32 = jnp.zeros((16, 128), F32)
    for s in range(32):
        a, b = gathered_ref[63 - 2 * s].astype(F32), gathered_ref[62 - 2 * s].astype(F32)
        top = jnp.where(low8, a, _roll(b))
        bottom = jnp.where(low8, _roll(a), b)
        coef[32 + s] = jnp.concatenate([top, bottom], axis=0).astype(BF)
    field[...] = jnp.zeros_like(field)
    copies[0].wait()
    size = 32
    while size >= 2:
        if size == 16:
            copies[1].wait()
        for s in range(size // 2, size):
            parts = []
            for h in (2 * s, 2 * s + 1):
                row = (2 * h - 2) * 64
                parts.append(_nn(coef[h], wide[row : row + 128, :]))
            coef[s] = jnp.where(low, parts[0], parts[1]).astype(BF)
        size //= 2
    copies[2].wait()
    copies[3].wait()
    for b in range(8):
        target = target_ref[b] if b < 4 else target2_ref[b - 4]
        source = source_ref[b] if b < 4 else source2_ref[b - 4]
        block = blocks_ref[b]
        block = jnp.concatenate([block, block], axis=0)
        block = jnp.concatenate([block, block], axis=1)
        x = _pick_half(low, source & 1, coef[source >> 1], zero)
        field[target >> 1] += _pick_half(low, target & 1, _nn(x, block), zero32)
    for h in range(2, 64):
        row = (2 * h - 2) * 64
        x = _pick_half(low, h % 2, field[h // 2].astype(BF), zero)
        field[h] += _nt(x, wide[row : row + 128, :])
    for s in range(32):
        x = field[32 + s]
        top, bottom = x[:8], x[8:]
        out_ref[63 - 2 * s] = jnp.where(low8, top, _roll(bottom)).astype(BF)
        out_ref[62 - 2 * s] = jnp.where(low8, _roll(top), bottom).astype(BF)


def near_kernel(
    me_ref, ids_ref, inner_hbm, own_hbm, own2_hbm, outer_hbm, blocks_hbm, mine_out, other_out, halo, own, blocks_ref, leaves, sems
):
    copies = _fetch(
        sems,
        (own_hbm, own.at[0:R]),
        (own2_hbm, own.at[R:]),
        (inner_hbm.at[64:128], halo.at[0]),
        (outer_hbm.at[64:128], halo.at[1]),
        *_chunks(blocks_hbm, blocks_ref, 2),
    )
    for copy in copies[:4]:
        copy.wait()
    core = me_ref[0] & 1
    for s in range(32):
        for part in range(3):
            if part == 1:
                z = own[:, 128 * s : 128 * s + 128]
            else:
                side = 1 - core if part == 0 else core
                z = jnp.concatenate([halo[side, s], halo[side, 32 + s]], axis=0)
            e = 64 * part + 2 * s
            leaves[e] = z[:, :64]
            leaves[e + 1] = z[:, 64:]
    start = (me_ref[0] - 1) * 64
    for p in range(32):
        if p % (32 // 2) == 0:
            copies[4 + p // (32 // 2)].wait()
        parts = []
        for i in (2 * p, 2 * p + 1):
            total = _nt(leaves[ids_ref[0, i] - start], blocks_ref[i, 0])
            for j in range(1, 4):
                total += _nt(leaves[ids_ref[j, i] - start], blocks_ref[i, j])
            parts.append(total)
        pair = jnp.concatenate(parts, axis=1)
        mine_out[:, 128 * p : 128 * p + 128] = pair[:R]
        other_out[:, 128 * p : 128 * p + 128] = pair[R:].astype(BF)


def field_kernel(me_ref, ids_ref, inner_hbm, own_hbm, outer_hbm, raw_hbm, out_ref, raw_ref, wide, seen, coef, sems):
    copies = _fetch(
        sems,
        (inner_hbm.at[0:64], seen.at[0]),
        (own_hbm.at[0:64], seen.at[1]),
        (outer_hbm.at[0:64], seen.at[2]),
        *[(raw_hbm.at[:, 32 * i : 32 * i + 32], raw_ref.at[:, 32 * i : 32 * i + 32]) for i in range(2)],
    )
    low = _low(R)
    core = me_ref[0] & 1
    for copy in copies[:3]:
        copy.wait()
    for part in range(3):
        side = (2 - 2 * core, 1, 2 * core)[part]
        for s in range(64):
            x = seen[side, s]
            y = jnp.concatenate([x[:, 64:], x[:, :64]], axis=1)
            coef[part * NODES + 2 * s] = jnp.where(low, x, y)
            coef[part * NODES + 2 * s + 1] = jnp.where(low, y, x)
    for m in range(64):
        if m % 32 == 0:
            copies[3 + m // 32].wait()
        for k in range(2):
            both = jnp.concatenate([raw_ref[k, m], raw_ref[k + 2, m]], axis=0).astype(F32)
            wide[pl.ds(k * 64 + m, raw_ref.shape[3], stride=PITCH_FIELD), :] = both.T
    before = me_ref[0] - 1

    def source(k, t):
        level = next(i for i in range(7) if t < FIRST[i] + SIZES[i])
        e = ids_ref[k, t] - before * SIZES[level]
        part = lax.shift_right_logical(e, 6 - level)
        return coef[part * NODES + (e & (SIZES[level] - 1)) + FIRST[level]]

    def node(t):
        a = jnp.where(low, source(0, t), source(1, t))
        b = jnp.where(low, source(2, t), source(3, t))
        y = _nn(jnp.concatenate([a, b], axis=0), wide[PITCH_FIELD * t : PITCH_FIELD * t + 128, :].astype(BF))
        return y[:R], y[R:]

    for s in range(63):
        a0, b0 = node(2 * s)
        a1, b1 = node(2 * s + 1)
        out_ref[s] = jnp.where(low, a0, b1) + _roll(jnp.where(low, a1, b0))
    a0, b0 = node(126)
    out_ref[63] = a0 + _roll(b0)


def down_kernel(me_ref, mine_ref, other_ref, field_ref, wide_ref, basis_ref, near_ref, near2_ref, out_ref, down):
    core = me_ref[0] & 1
    low = _low(R)
    zero = jnp.zeros((R, 128), BF)
    first = jnp.where(core == 0, mine_ref[...], other_ref[...])
    second = jnp.where(core == 0, other_ref[...], mine_ref[...])
    upper = jnp.concatenate([first, _roll(first), second, _roll(second)], axis=0)
    upper = jnp.where(low, upper, 0.0).astype(BF)
    root = field_ref[63][:, :64] + _nt(upper, wide_ref[126 * 64 : 127 * 64, :])
    down[63] = jnp.concatenate([root, root], axis=1).astype(BF)
    for level in range(5, -1, -1):
        for q in range(SIZES[level + 1]):
            row = (FIRST[level] + 2 * q) * 64
            x = _pick_half(low, q % 2, down[SLOT[level + 1] + q // 2], zero)
            s = SLOT[level] + q
            down[s] = (field_ref[s] + _nt(x, wide_ref[row : row + 128, :])).astype(BF)
    for p in range(32):
        d = down[p]
        both = jnp.concatenate([d[:, :64], d[:, 64:]], axis=0)
        y = _nt(both, basis_ref[2 * p : 2 * p + 2].reshape(128, 64))
        lanes = slice(128 * p, 128 * p + 128)
        total = jnp.where(low, y[:R], y[R:]) + near_ref[:, lanes] + near2_ref[:, lanes].astype(F32)
        out_ref[:, lanes] = total.astype(BF)


def _call(body, name, outs, ins, scratch, limit, micros, out_specs=None, aliases={}):
    vm = pl.BlockSpec(memory_space=pltpu.VMEM)
    if out_specs is None:
        out_specs = (vm,) * len(outs) if isinstance(outs, tuple) else vm
    return pl.pallas_call(
        body,
        out_shape=outs,
        in_specs=ins,
        out_specs=out_specs,
        scratch_shapes=scratch,
        input_output_aliases=aliases,
        compiler_params=pltpu.CompilerParams(vmem_limit_bytes=limit * MIB),
        cost_estimate=pl.CostEstimate(
            flops=int(micros * 1.0e9), bytes_accessed=int(micros * 3.0e6), transcendentals=0
        ),
        name=name,
    )


def shards(
    vectors,
    leaf_basis,
    local_transfer,
    coupling,
    coupling_source,
    top_transfer,
    top_coupling,
    top_target,
    top_source,
    near_blocks,
    near_source,
):
    n_leaf = lax.axis_size("leaf")
    me = lax.axis_index("leaf").astype(jnp.int32).reshape(1)
    vm = pl.BlockSpec(memory_space=pltpu.VMEM)
    sm = pl.BlockSpec(memory_space=pltpu.SMEM)
    S = jax.ShapeDtypeStruct
    pair = [(i, i ^ 1) for i in range(n_leaf)]
    across = [(i, i + 1) for i in range(1, n_leaf - 1, 2)]
    across += [(j, i) for i, j in across]
    swap = [(0, 1), (1, 0)]
    groups = [[2 * i + c for i in reversed(range(n_leaf // 2))] for c in range(2)]

    hbm = pl.BlockSpec(memory_space=pltpu.HBM)
    any_ = pl.BlockSpec(memory_space=pl.ANY)
    dma = pltpu.SemaphoreType.DMA
    V = pltpu.VMEM
    raw = jnp.transpose(local_transfer, (1, 2, 0))
    msg, root, wide = _call(
        up_kernel,
        "up",
        (S((128, R, 128), BF), S((R, 128), F32), S((NODES * 64, 128), BF)),
        [hbm, hbm, hbm],
        [
            V(vectors.shape, BF),
            V(leaf_basis.shape, BF),
            V(raw.shape, BF),
            V((96, R, 128), BF),
            V((NODES * PITCH, 128), F32),
            V((NODES * 64, 128), BF),
            dma((4,)),
            dma((4,)),
        ],
        59,
        4,
        (hbm, vm, hbm),
    )(vectors, leaf_basis, raw)

    root2 = lax.ppermute(root, "leaf", pair)
    send = _call(pack_kernel, "pack", S((n_leaf // 2, 8, 128), BF), [sm, vm, vm], [], 4, 0.5)(
        me, root, root2
    )
    gathered = lax.all_to_all(send, "leaf", 0, 0, tiled=True, axis_index_groups=groups)
    vectors2 = lax.ppermute(vectors, "rhs", swap)
    block, target, source, _ = lax.optimization_barrier(
        (top_coupling, top_target, top_source, send)
    )
    top_coupling2 = lax.ppermute(block, "leaf", pair)
    top_target2 = lax.ppermute(target, "leaf", pair)
    top_source2 = lax.ppermute(source, "leaf", pair)

    raw = jnp.transpose(top_transfer, (1, 2, 0))
    wide_top, msg = _call(
        top_kernel,
        "top",
        (S((NODES * 64, 128), BF), S((128, R, 128), BF)),
        [hbm] + [any_] * 5,
        [
            V(raw.shape, BF),
            V((NODES * PITCH, 128), F32),
            V((NODES * 64, 128), BF),
            dma((2,)),
            dma((1,)),
        ],
        57,
        4,
        (hbm, any_),
        {1: 1},
    )(raw, msg, send, top_coupling2, top_target2, top_source2)

    msg = pl.pallas_call(
        bundle_kernel,
        grid=(1,),
        out_shape=S((128, R, 128), BF),
        in_specs=[any_, vm, any_],
        out_specs=pl.BlockSpec((32, R, 128), lambda i: (3, 0, 0)),
        input_output_aliases={0: 0},
        compiler_params=pltpu.CompilerParams(vmem_limit_bytes=4 * MIB),
        cost_estimate=pl.CostEstimate(flops=0, bytes_accessed=1000000, transcendentals=0),
        name="bundle",
    )(msg, vectors2, gathered)
    inner = lax.ppermute(msg, "leaf", pair)
    outer = lax.ppermute(msg, "leaf", across)
    partial = _call(
        upper_kernel,
        "upper",
        S((n_leaf // 2, 8, 128), BF),
        [sm, sm, sm, sm, vm, hbm, any_, any_],
        [
            V((NODES * 64, 128), BF),
            V((8, 64, 64), BF),
            V((64, 16, 128), BF),
            V((64, 16, 128), F32),
            dma((4,)),
        ],
        57,
        6,
    )(top_target, top_source, top_target2, top_source2, gathered, wide_top, top_coupling, top_coupling2)
    parts = lax.all_to_all(partial, "leaf", 0, 0, tiled=True, axis_index_groups=groups)

    near_mine, near_send = _call(
        near_kernel,
        "near",
        (S((R, 4096), F32), S((R, 4096), BF)),
        [sm, sm, any_, any_, any_, any_, hbm],
        [
            V((2, 64, R, 128), BF),
            V((2 * R, 4096), BF),
            V(near_blocks.shape, BF),
            V((192, 64, 64), BF),
            dma((12,)),
        ],
        49,
        5,
    )(me, near_source.T, inner, vectors, vectors2, outer, near_blocks)
    near_other = lax.ppermute(near_send, "rhs", swap)
    parts, near_mine = lax.optimization_barrier((parts, near_mine))
    mine = _call(sum_kernel, "total", S((8, 128), F32), [vm], [], 4, 0.5)(parts)
    other = lax.ppermute(mine, "leaf", pair)

    raw = jnp.transpose(coupling, (1, 2, 3, 0))
    fields = _call(
        field_kernel,
        "field",
        S((64, R, 128), F32),
        [sm, sm, any_, any_, any_, hbm],
        [
            V(raw.shape, BF),
            V((NODES * PITCH_FIELD, 128), F32),
            V((3, 64, R, 128), BF),
            V((3 * NODES, R, 128), BF),
            dma((5,)),
        ],
        49,
        2,
    )(me, coupling_source.T, inner, msg, outer, raw)

    return _call(
        down_kernel,
        "down",
        S((R, 4096), BF),
        [sm] + [vm] * 7,
        [V((64, R, 128), BF)],
        10,
        4,
    )(me, mine, other, fields, wide, leaf_basis, near_mine, near_other)


def solution(mesh):
    placed = (
        P("rhs", "leaf"),
        P("leaf", None, None),
        P("leaf", None, None),
        P("leaf", None, None, None),
        P("leaf", None),
        P(),
        P("leaf", None, None),
        P("leaf"),
        P("leaf"),
        P("leaf", "rhs", None, None),
        P("leaf", "rhs"),
    )
    return jax.shard_map(
        shards, mesh=mesh, in_specs=placed, out_specs=P("rhs", "leaf"), check_vma=False
    )
```
